256 devices in a mesh: section: 2 (over y_lo), fsdp: 32 (over z, y_hi, core), seq: 4 (over x).
Axes of the slice: x: 4, y: 4 (y_hi: 2, y_lo: 2; y = y_hi * 2 + y_lo), z: 8, core: 2. Of those that a mesh axis runs over, the one named last changes fastest.
Arguments:
- inputs: bfloat16 [2, 4, 6144, 4096], P('section', None, 'fsdp', 'seq'), may hold values from -6 to 6
- gains: float32 [2, 4096], P('section'), may hold values from 0.25 to 1.75
- weights: bfloat16 [2, 4096, 2, 4096], P('section', 'fsdp', None, 'seq'), may hold values from -0.09375 to 0.09375
- lengths: int32 [4, 32], P(None, 'fsdp'), may hold values from 1 to 192
Outputs:
- section_outputs: bfloat16 [2, 4, 6144, 2, 4096], P('section', None, 'fsdp', None, 'seq')
The draws below stay inside these ranges and needn't reach their ends.
All inputs are finite; a program needn't handle non-finite values.
Results may differ from the reference program's by a relative error of at most 0.005.
Values may be sent and summed in bfloat16 or wider, within the bound.
No kernel may reach another device: no remote copies, remote signals or barrier semaphores. Data moves between devices by JAX's collectives and lax.ppermute only.
A program may use at most 128 MiB of HBM per device.

```python
import jax
import jax.numpy as jnp
from jax import lax

D = 4096
HEADS = 64
HD = 64
TOK_DEV = 192
MB = 4
WINDOWS = 32
TOKENS = 6144


def plant(array, own_key, low, high):
    longest = array.shape.index(max(array.shape))
    spots = []
    for shift in (0, 1):
        where = [jax.random.randint(jax.random.fold_in(own_key, axis), (), 0, length) for axis, length in enumerate(array.shape)]
        where[longest] = (where[longest] + shift) % array.shape[longest]
        spots.append(tuple(where))
    return array.at[spots[0]].set(low).at[spots[1]].set(high)


def steps_of(rng, dims, cuts, least, high):
    def one(axis_at, blocks):
        steps = jax.random.uniform(jax.random.fold_in(jax.random.fold_in(rng, 6), axis_at), (blocks,), jnp.float32, least / len(cuts), high / len(cuts))
        return jnp.repeat(jnp.exp(steps), dims[axis_at] // blocks).reshape((-1,) + (1,) * (len(dims) - axis_at - 1))

    level = one(*cuts[0])
    for cut in cuts[1:]:
        level = level * one(*cut)
    return level


def centred(rng, shape, spread, most, shards=(), kind=jnp.bfloat16):
    gain = steps_of(rng, shape, shards, -0.22, 0.18) if shards else 1.0
    drawn = jax.random.normal(rng, shape, jnp.float32) * spread * gain
    return jnp.minimum(jnp.maximum(drawn, -most), most).astype(kind)


def setup_inputs(seed: int = 0) -> dict:
    streams_of = jax.random.split(jax.random.key(seed), 5)
    return {
        "inputs": centred(streams_of[0], (2, MB, TOKENS, D), 1.0, 6.0, ((0, 2), (2, 32), (3, 4))),
        "gains": jnp.clip(1.0 + 0.15 * jax.random.normal(streams_of[1], (2, D), jnp.float32), 0.25, 1.75),
        "weights": centred(streams_of[2], (2, D, 2, D), D ** -0.5, 0.09375, ((0, 2), (1, 32), (3, 4))),
        "lengths": plant(jax.random.randint(streams_of[3], (MB, WINDOWS), 1, TOK_DEV + 1), jax.random.fold_in(streams_of[3], 1), 1, TOK_DEV).astype(jnp.int32),
    }


def reference(inputs, gains, weights, lengths):
    x = inputs.astype(jnp.float32)
    mean_sq = lax.optimization_barrier(jnp.mean(x * x, axis=-1, keepdims=True))
    normed = (x * lax.rsqrt(mean_sq + 1e-06) * gains[:, None, None, :]).astype(jnp.bfloat16)

    def project(section_pair):
        rows, weight = section_pair
        flat = rows.reshape(MB * TOKENS, D)
        out = jnp.dot(flat, weight.reshape(D, 2 * D), preferred_element_type=jnp.float32)
        return out.astype(jnp.bfloat16).reshape(MB, TOKENS, 2, D)
    projected = lax.map(project, (normed, weights))
    query = projected[1, :, :, 0].reshape(MB, WINDOWS, TOK_DEV, HEADS, HD)
    gate = projected[1, :, :, 1].reshape(MB, WINDOWS, TOK_DEV, D)
    key = projected[0, :, :, 0].reshape(MB, WINDOWS, TOK_DEV, HEADS, HD)
    value = projected[0, :, :, 1].reshape(MB, WINDOWS, TOK_DEV, HEADS, HD)

    def window(args):
        q_win, k_win, v_win, g_win, limit = args
        scores = jnp.einsum('mqhe,mkhe->mhqk', q_win.astype(jnp.float32), k_win.astype(jnp.float32)) / jnp.sqrt(jnp.float32(HD))
        place = jnp.arange(TOK_DEV, dtype=jnp.int32)
        valid = place[None, None, None, :] < limit[:, None, None, None]
        scores = jnp.where(valid, scores, jnp.float32(-1e+30))
        probs = jax.nn.softmax(scores, axis=-1).astype(jnp.bfloat16)
        context = jnp.einsum('mhqk,mkhe->mqhe', probs.astype(jnp.float32), v_win.astype(jnp.float32))
        context = context.reshape(MB, TOK_DEV, D)
        return (jax.nn.sigmoid(g_win.astype(jnp.float32)) * context).astype(jnp.bfloat16)
    moved = (jnp.swapaxes(query, 0, 1), jnp.swapaxes(key, 0, 1), jnp.swapaxes(value, 0, 1), jnp.swapaxes(gate, 0, 1), jnp.swapaxes(lengths, 0, 1))
    attended = lax.map(window, moved)
    attended = jnp.swapaxes(attended, 0, 1).reshape(MB, TOKENS, D)
    return projected.at[1, :, :, 0].set(attended)
```

```python
import functools

import jax
import jax.numpy as jnp
import numpy as np
from jax import lax
from jax.experimental import pallas as pl
from jax.experimental.pallas import tpu as pltpu
from jax.sharding import PartitionSpec as P

HD = 64
AXES = ("section", "fsdp", "seq")
ROWS = 128
BIG = 56 * 1024 * 1024


def pairs_of(rule):
    pairs = []
    for s in range(2):
        for z in range(8):
            for y in range(2):
                for c in range(2):
                    for x in range(4):
                        to = rule(s, z, y, c, x)
                        if to is not None:
                            number = lambda s, z, y, c, x: s * 128 + z % 8 * 16 + y * 8 + c * 4 + x % 4
                            pairs.append((number(s, z, y, c, x), number(*to)))
    return pairs


Z_UP = pairs_of(lambda s, z, y, c, x: (s, z + 1, y, c, x))
Z_DOWN = pairs_of(lambda s, z, y, c, x: (s, z - 1, y, c, x))
Y_OTHER = pairs_of(lambda s, z, y, c, x: (s, z, 1 - y, c, x))
CORE_OTHER = pairs_of(lambda s, z, y, c, x: (s, z, y, 1 - c, x))
X_RING = pairs_of(lambda s, z, y, c, x: (s, z, y, c, x + 1 - 2 * c))
TO_ENC = pairs_of(lambda s, z, y, c, x: (0, z, y, c, x) if s == 1 else None)
TO_DEC = pairs_of(lambda s, z, y, c, x: (1, z, y, c, x) if s == 0 else None)


def sent(x, pairs):
    return lax.ppermute(x, AXES, pairs)


def after(x, *others):
    return lax.optimization_barrier((x, *others))[0]


def rows(*parts):
    return jnp.concatenate(parts, axis=0)


LAST = [(0, 6), (0, 3), (0, 4)]
FIRST = [(1, 0), (1, 7), (1, 1), (1, 6), (1, 2)]
SECOND = [(1, 5), (1, 3), (0, 0), (0, 7), (0, 1)]
THIRD = [(1, 4), (0, 2), (0, 5)]
PLACE = np.zeros((2, 2, 8), np.int32)
_at = 0
for _bundle in (LAST, FIRST, SECOND, THIRD):
    for _own in (1, 0):
        for _same, _far in _bundle:
            PLACE[_same, _own, _far] = _at
            _at += 1


def norm_kernel(source_ref, place_ref, gain_ref, x0, x1, x2, x3, out_ref):
    slices = (x0, x1, x2, x3)
    total = 0.0
    for ref in slices:
        v = ref[...].astype(jnp.float32)
        total = total + jnp.sum(v * v, axis=-1, keepdims=True)
    scale = lax.rsqrt(total / 4096 + 1e-06)
    for i, ref in enumerate(slices):
        gain = gain_ref[:, pl.ds(pl.multiple_of(source_ref[i] * 1024, 1024), 1024)]
        normed = (ref[...].astype(jnp.float32) * scale * gain).astype(jnp.bfloat16)
        for b in range(8):
            at = pl.multiple_of(place_ref[i * 8 + b] * ROWS, ROWS)
            out_ref[:, pl.ds(at, ROWS)] = normed[:, b * ROWS:(b + 1) * ROWS]


def norm(source, place, gains, slices):
    tokens = slices[0].shape[0]
    step = 96
    return pl.pallas_call(
        norm_kernel,
        grid_spec=pltpu.PrefetchScalarGridSpec(
            num_scalar_prefetch=2,
            grid=(tokens // step,),
            in_specs=[pl.BlockSpec((1, 4096), lambda i, *_: (0, 0))]
            + [pl.BlockSpec((step, 1024), lambda i, *_: (i, 0))] * 4,
            out_specs=pl.BlockSpec((step, 4096), lambda i, *_: (i, 0)),
        ),
        out_shape=jax.ShapeDtypeStruct((tokens, 4096), jnp.bfloat16),
        compiler_params=pltpu.CompilerParams(vmem_limit_bytes=BIG),
        cost_estimate=pl.CostEstimate(flops=tokens * 4096 * 6, bytes_accessed=tokens * 4096 * 4, transcendentals=tokens),
    )(source, place, gains, *slices)


def matmul_kernel(depths, start, n_in, x_ref, *refs):
    out_ref = refs[-1]
    total = refs[n_in - 1][...] if n_in > len(depths) else None
    at = start
    for ref, depth in zip(refs, depths):
        part = jnp.dot(x_ref[:, at:at + depth], ref[...], preferred_element_type=jnp.float32)
        total = part if total is None else total + part
        at += depth
    out_ref[...] = total.astype(out_ref.dtype)


def matmul(x, x_block, start, parts, base, dtype, width, column, tile=256):
    tokens = x.shape[0]
    depths = [p.shape[0] for p in parts]
    first = column // tile
    in_specs = [pl.BlockSpec((tokens, x_block), lambda j: (0, 0))]
    in_specs += [pl.BlockSpec((d, tile), lambda j: (0, first + j)) for d in depths]
    args = [x, *parts]
    if base is not None:
        in_specs.append(pl.BlockSpec((tokens, tile), lambda j: (0, first + j)))
        args.append(base)
    return pl.pallas_call(
        functools.partial(matmul_kernel, depths, start, len(args) - 1),
        grid=(width // tile,),
        in_specs=in_specs,
        out_specs=pl.BlockSpec((tokens, tile), lambda j: (0, j)),
        out_shape=jax.ShapeDtypeStruct((tokens, width), dtype),
        compiler_params=pltpu.CompilerParams(vmem_limit_bytes=BIG),
        cost_estimate=pl.CostEstimate(
            flops=2 * tokens * sum(depths) * width,
            bytes_accessed=2 * (tokens + width) * sum(depths) + 6 * tokens * width,
            transcendentals=0,
        ),
    )(*args)


def attend_kernel(index, limit_ref, q_ref, k_ref, v_ref, out_ref):
    tok, width = q_ref.shape
    valid = lax.broadcasted_iota(jnp.int32, (tok, tok), 1) < limit_ref[index]
    low = lax.broadcasted_iota(jnp.int32, (tok, 2 * HD), 1) < HD
    for pair in range(width // (2 * HD)):
        cols = slice(pair * 2 * HD, (pair + 1) * 2 * HD)
        q, k, v = q_ref[:, cols], k_ref[:, cols], v_ref[:, cols]
        halves = []
        for mine in (low, ~low):
            scores = lax.dot_general(
                jnp.where(mine, q, jnp.zeros_like(q)), k, (((1,), (1,)), ((), ())), preferred_element_type=jnp.float32
            ) * 0.125
            scores = jnp.where(valid, scores, jnp.float32(-1e30))
            top = jnp.max(scores, axis=-1, keepdims=True)
            e = jnp.exp(scores - top)
            probs = (e * (1.0 / jnp.sum(e, axis=-1, keepdims=True))).astype(jnp.bfloat16)
            halves.append(jnp.dot(probs, v, preferred_element_type=jnp.float32))
        out_ref[:, cols] = jnp.where(low, halves[0], halves[1]).astype(out_ref.dtype)


def attend(index, limit, q, k, v):
    tok, width = q.shape
    return pl.pallas_call(
        functools.partial(attend_kernel, index),
        grid_spec=pltpu.PrefetchScalarGridSpec(
            num_scalar_prefetch=1,
            grid=(1,),
            in_specs=[
                pl.BlockSpec((tok, width), lambda i, *_: (0, 0)),
                pl.BlockSpec((tok, width), lambda i, *_: (index, 0)),
                pl.BlockSpec((tok, width), lambda i, *_: (index, 0)),
            ],
            out_specs=pl.BlockSpec((tok, width), lambda i, *_: (0, 0)),
        ),
        out_shape=jax.ShapeDtypeStruct((tok, width), jnp.bfloat16),
        compiler_params=pltpu.CompilerParams(vmem_limit_bytes=BIG),
        cost_estimate=pl.CostEstimate(
            flops=4 * tok * tok * width * 2, bytes_accessed=8 * tok * width, transcendentals=tok * tok * width // HD
        ),
    )(limit, q, k, v)


def per_device(inputs, gains, weights, lengths):
    _, batch, tok, wide = inputs.shape
    fsdp, seq = lax.axis_index("fsdp"), lax.axis_index("seq")
    z, y, core = fsdp // 4, fsdp // 2 % 2, fsdp % 2
    is_decoder = lax.axis_index("section") == 1

    steps = np.arange(4, dtype=np.int32)
    source = (seq + (2 * core - 1) * steps) % 4
    block = (source[:, None] * 8 + np.arange(8, dtype=np.int32)[None, :]).reshape(32)
    same = (block // 2 % 2 == y).astype(jnp.int32)
    own = (block % 2 == core).astype(jnp.int32)
    place = jnp.asarray(PLACE).reshape(32)[(same * 2 + own) * 8 + (block // 4 - z) % 8]

    x0 = inputs.reshape(batch * tok, wide)
    w0 = weights.reshape(ROWS, 2 * wide)

    up1, down1 = sent(w0, Z_UP), sent(w0, Z_DOWN)
    other0 = sent(w0, Y_OTHER)
    x1 = sent(x0, X_RING)

    up2, down2 = sent(up1, Z_UP), sent(down1, Z_DOWN)
    other1 = sent(rows(up1, down1), Y_OTHER)
    x2 = sent(x1, X_RING)

    first = rows(w0, up1, down1, up2, down2)
    first_o = sent(first, CORE_OTHER)
    up3, down3 = sent(after(up2, x1, other0), Z_UP), sent(down2, Z_DOWN)
    x3 = sent(x2, X_RING)

    up4 = sent(after(up3, x2, first_o), Z_UP)
    p_down2 = sent(other1[ROWS:], Z_DOWN)
    other3 = sent(up3, Y_OTHER)
    second = rows(up3, down3, other0, other1)
    second_o = sent(second, CORE_OTHER)

    p_up2 = sent(after(other1[:ROWS], up4, x3, second_o), Z_UP)
    p_down3 = sent(p_down2, Z_DOWN)
    other4 = sent(after(up4, other3), Y_OTHER)
    third = rows(up4, p_down2, other3)
    third_o = sent(third, CORE_OTHER)

    normed = norm(source, place, gains, (x0, x1, x2, x3))
    begun = matmul(
        normed, 4096, 6 * ROWS, (first, first_o, second, second_o, third, third_o), None, jnp.float32, 2 * wide, 0
    )

    last = rows(p_up2, p_down3, other4)
    last_o = sent(last, CORE_OTHER)
    front = matmul(normed, 6 * ROWS, 0, (last, last_o), begun, jnp.bfloat16, wide, 0, 512)
    queries = [sent(front[i * tok:(i + 1) * tok], TO_ENC) for i in range(batch)]
    back = matmul(normed, 6 * ROWS, 0, (last, last_o), begun, jnp.bfloat16, wide, wide, 512)

    limit = lengths.reshape(batch)
    context = [sent(attend(i, limit, queries[i], front, back), TO_DEC) for i in range(batch)]
    context = rows(*context).astype(jnp.float32)
    attended = (jax.nn.sigmoid(back.astype(jnp.float32)) * context).astype(jnp.bfloat16)
    final = jnp.stack([jnp.where(is_decoder, attended, front), back], axis=1)
    return final.reshape(1, batch, tok, 2, wide)


def solution(mesh):
    in_specs = (
        P("section", None, "fsdp", "seq"),
        P("section", None),
        P("section", "fsdp", None, "seq"),
        P(None, "fsdp"),
    )
    out_specs = P("section", None, "fsdp", None, "seq")
    return jax.shard_map(
        per_device, mesh=mesh, in_specs=in_specs, out_specs=out_specs, check_vma=False
    )
```

```python
import functools

import jax
import jax.numpy as jnp
import numpy as np
from jax import lax
from jax.experimental import pallas as pl
from jax.experimental.pallas import tpu as pltpu
from jax.sharding import PartitionSpec as P

HD = 64
AXES = ("section", "fsdp", "seq")
ROWS = 128
MIB = 1024 * 1024


def pairs_of(rule):
    pairs = []
    for s in range(2):
        for z in range(8):
            for y in range(2):
                for c in range(2):
                    for x in range(4):
                        to = rule(s, z, y, c, x)
                        if to is not None:
                            number = lambda s, z, y, c, x: s * 128 + z % 8 * 16 + y * 8 + c * 4 + x % 4
                            pairs.append((number(s, z, y, c, x), number(*to)))
    return pairs


Z_UP = pairs_of(lambda s, z, y, c, x: (s, z + 1, y, c, x))
Z_DOWN = pairs_of(lambda s, z, y, c, x: (s, z - 1, y, c, x))
Y_OTHER = pairs_of(lambda s, z, y, c, x: (s, z, 1 - y, c, x))
CORE_OTHER = pairs_of(lambda s, z, y, c, x: (s, z, y, 1 - c, x))
X_RING = pairs_of(lambda s, z, y, c, x: (s, z, y, c, x + 1 - 2 * c))
TO_ENC = pairs_of(lambda s, z, y, c, x: (0, z, y, c, x) if s == 1 else None)
TO_DEC = pairs_of(lambda s, z, y, c, x: (1, z, y, c, x) if s == 0 else None)


def sent(x, pairs):
    return lax.ppermute(x, AXES, pairs)


def after(x, *others):
    return lax.optimization_barrier((x, *others))[0]


def stack_kernel(*refs):
    parts, out, done = refs[:-2], refs[-2], refs[-1]
    copies, at = [], 0
    for k, part in enumerate(parts):
        copies.append(pltpu.make_async_copy(part, out.at[pl.ds(at, part.shape[0])], done.at[k]))
        at += part.shape[0]
    for copy in copies:
        copy.start()
    for copy in copies:
        copy.wait()


def stacked(*parts):
    return pl.pallas_call(
        stack_kernel,
        in_specs=[pl.BlockSpec(memory_space=pl.ANY)] * len(parts),
        out_specs=pl.BlockSpec(memory_space=pl.ANY),
        out_shape=jax.ShapeDtypeStruct((sum(p.shape[0] for p in parts), parts[0].shape[1]), parts[0].dtype),
        scratch_shapes=[pltpu.SemaphoreType.DMA((len(parts),))],
        compiler_params=pltpu.CompilerParams(vmem_limit_bytes=MIB),
        cost_estimate=pl.CostEstimate(flops=0, bytes_accessed=1024, transcendentals=0),
    )(*parts)


LAST = [(0, 6), (0, 3), (0, 4)]
FIRST = [(1, 0), (1, 7), (1, 1), (1, 6), (1, 2)]
SECOND = [(1, 5), (1, 3), (0, 0), (0, 1), (0, 7)]
THIRD = [(1, 4), (0, 2), (0, 5)]
PLACE = np.zeros((2, 2, 8), np.int32)
_at = 0
for _bundle in (LAST, FIRST, SECOND, THIRD):
    for _own in (1, 0):
        for _same, _far in _bundle:
            PLACE[_same, _own, _far] = _at
            _at += 1


def norm_kernel(group, place_ref, gain_ref, x_ref, out_ref):
    places = [pl.multiple_of(place_ref[k] * ROWS, ROWS) for k in range(32)]

    @pl.loop(0, x_ref.shape[0] // group, unroll=True)
    def _(g):
        at = pl.ds(g * group, group)
        values = [x_ref[at, i * 1024:(i + 1) * 1024].astype(jnp.float32) for i in range(4)]
        squares = (values[0] * values[0] + values[1] * values[1]) + (values[2] * values[2] + values[3] * values[3])
        scale = lax.rsqrt(jnp.sum(squares, axis=-1, keepdims=True) / 4096 + 1e-06)
        for i in range(4):
            normed = (values[i] * scale * gain_ref[:, i * 1024:(i + 1) * 1024]).astype(jnp.bfloat16)
            for b in range(8):
                out_ref[at, pl.ds(places[i * 8 + b], ROWS)] = normed[:, b * ROWS:(b + 1) * ROWS]


def norm(place, gains, x):
    tokens, width = x.shape
    step = 64
    return pl.pallas_call(
        functools.partial(norm_kernel, 32),
        grid_spec=pltpu.PrefetchScalarGridSpec(
            num_scalar_prefetch=1,
            grid=(tokens // step,),
            in_specs=[
                pl.BlockSpec((1, width), lambda i, *_: (0, 0)),
                pl.BlockSpec((step, width), lambda i, *_: (i, 0)),
            ],
            out_specs=pl.BlockSpec((step, width), lambda i, *_: (i, 0)),
        ),
        out_shape=jax.ShapeDtypeStruct((tokens, width), jnp.bfloat16),
        compiler_params=pltpu.CompilerParams(vmem_limit_bytes=6 * MIB),
        cost_estimate=pl.CostEstimate(
            flops=tokens * width * 6, bytes_accessed=tokens * width * 4, transcendentals=tokens
        ),
    )(place, gains, x)


def matmul_kernel(start, n_x, n_parts, has_base, tile, pieces, *refs):
    xs, parts = refs[:n_x], refs[n_x:n_x + n_parts]
    outs, held = refs[n_x + n_parts + has_base:-1], refs[-1]
    j = pl.program_id(0)
    depth = 0
    for part in parts:
        held[depth:depth + part.shape[0], :] = part[...]
        depth += part.shape[0]
    row = 0
    for x in xs:
        count = x.shape[0]
        total = jnp.dot(x[:, start:start + depth], held[...], preferred_element_type=jnp.float32)
        if has_base:
            total = total + refs[n_x + n_parts][row:row + count, :]
        for (low, high, left, right), out in zip(pieces, outs):
            begin, end = max(low, row), min(high, row + count)
            if begin < end:

                @pl.when((j >= left // tile) & (j < right // tile))
                def _():
                    out[begin - low:end - low, :] = total[begin - row:end - row].astype(out.dtype)
        row += count


def matmul(xs, x_block, start, parts, base, dtype, width, column, tile, pieces, mib, weight=1):
    tokens = sum(x.shape[0] for x in xs)
    depths = [p.shape[0] for p in parts]
    first = column // tile
    in_specs = [pl.BlockSpec((x.shape[0], x_block), lambda j: (0, 0), pipeline_mode=pl.Buffered(1)) for x in xs]
    in_specs += [pl.BlockSpec((d, tile), lambda j: (0, first + j)) for d in depths]
    args = [*xs, *parts]
    if base is not None:
        in_specs.append(pl.BlockSpec((tokens, tile), lambda j: (0, first + j)))
        args.append(base)

    def placed(left, right):
        return lambda j: (0, jnp.clip(j - left // tile, 0, (right - left) // tile - 1))

    return pl.pallas_call(
        functools.partial(matmul_kernel, start, len(xs), len(parts), base is not None, tile, pieces),
        grid=(width // tile,),
        in_specs=in_specs,
        out_specs=[pl.BlockSpec((high - low, tile), placed(left, right)) for low, high, left, right in pieces],
        out_shape=[jax.ShapeDtypeStruct((high - low, right - left), dtype) for low, high, left, right in pieces],
        scratch_shapes=[pltpu.VMEM((sum(depths), tile), jnp.bfloat16)],
        compiler_params=pltpu.CompilerParams(vmem_limit_bytes=mib * MIB),
        cost_estimate=pl.CostEstimate(
            flops=weight * 2 * tokens * sum(depths) * width,
            bytes_accessed=weight * (2 * (tokens + width) * sum(depths) + 6 * tokens * width),
            transcendentals=0,
        ),
    )(*args)


def attend_kernel(index, limit_ref, q_ref, k_ref, v_ref, out_ref):
    tok, width = q_ref.shape
    valid = lax.broadcasted_iota(jnp.int32, (tok, tok), 1) < limit_ref[index]
    low = lax.broadcasted_iota(jnp.int32, (tok, 2 * HD), 1) < HD
    for pair in range(width // (2 * HD)):
        cols = slice(pair * 2 * HD, (pair + 1) * 2 * HD)
        q, k, v = q_ref[:, cols], k_ref[:, cols], v_ref[:, cols]
        halves = []
        for mine in (low, ~low):
            scores = lax.dot_general(
                jnp.where(mine, q, jnp.zeros_like(q)), k, (((1,), (1,)), ((), ())), preferred_element_type=jnp.float32
            ) * 0.125
            scores = jnp.where(valid, scores, jnp.float32(-1e30))
            top = jnp.max(scores, axis=-1, keepdims=True)
            e = jnp.exp(scores - top)
            probs = (e * (1.0 / jnp.sum(e, axis=-1, keepdims=True))).astype(jnp.bfloat16)
            halves.append(jnp.dot(probs, v, preferred_element_type=jnp.float32))
        out_ref[:, cols] = jnp.where(low, halves[0], halves[1]).astype(out_ref.dtype)


def attend(index, limit, q, k, v):
    tok, width = q.shape
    whole = pl.BlockSpec((tok, width), lambda i, *_: (0, 0))
    return pl.pallas_call(
        functools.partial(attend_kernel, index),
        grid_spec=pltpu.PrefetchScalarGridSpec(
            num_scalar_prefetch=1, grid=(1,), in_specs=[whole, whole, whole], out_specs=whole
        ),
        out_shape=jax.ShapeDtypeStruct((tok, width), jnp.bfloat16),
        compiler_params=pltpu.CompilerParams(vmem_limit_bytes=8 * MIB),
        cost_estimate=pl.CostEstimate(
            flops=4 * tok * tok * width * 2, bytes_accessed=8 * tok * width, transcendentals=tok * tok * width // HD
        ),
    )(limit, q, k, v)


def finish_kernel(decoder_ref, front_ref, back_ref, context_ref, *refs):
    out_ref = refs[-1]

    @pl.when(decoder_ref[0] == 1)
    def _():
        gate = jax.nn.sigmoid(back_ref[...].astype(jnp.float32))
        out_ref[0, 0, :, 0, :] = (gate * context_ref[...].astype(jnp.float32)).astype(out_ref.dtype)

    @pl.when(decoder_ref[0] != 1)
    def _():
        out_ref[0, 0, :, 0, :] = front_ref[...]

    out_ref[0, 0, :, 1, :] = back_ref[...]


def finish(index, column, shape, decoder, front, back, context, begun):
    tok, width = front.shape
    step = tok // 2
    part = pl.BlockSpec((step, width), lambda i, *_: (i, 0))
    args, in_specs, aliases = [front, back, context], [part, part, part], {}
    if begun is not None:
        args.append(begun)
        in_specs.append(pl.BlockSpec(memory_space=pl.ANY))
        aliases = {4: 0}
    return pl.pallas_call(
        finish_kernel,
        grid_spec=pltpu.PrefetchScalarGridSpec(
            num_scalar_prefetch=1,
            grid=(2,),
            in_specs=in_specs,
            out_specs=pl.BlockSpec((1, 1, step, 2, width), lambda i, *_: (0, index, i, 0, column // width)),
        ),
        out_shape=jax.ShapeDtypeStruct(shape, jnp.bfloat16),
        input_output_aliases=aliases,
        compiler_params=pltpu.CompilerParams(vmem_limit_bytes=6 * MIB),
        cost_estimate=pl.CostEstimate(flops=6 * tok * width, bytes_accessed=10 * tok * width, transcendentals=tok * width),
    )(decoder, *args)


def per_device(inputs, gains, weights, lengths):
    _, batch, tok, wide = inputs.shape
    fsdp, seq = lax.axis_index("fsdp"), lax.axis_index("seq")
    z, y, core = fsdp // 4, fsdp // 2 % 2, fsdp % 2
    decoder = lax.axis_index("section").astype(jnp.int32).reshape(1)

    block = np.arange(32, dtype=np.int32)
    same = (block // 2 % 2 == y).astype(jnp.int32)
    own = (block % 2 == core).astype(jnp.int32)
    place = jnp.asarray(PLACE).reshape(32)[(same * 2 + own) * 8 + (block // 4 - z) % 8]

    x = lax.all_gather(inputs, "seq", axis=3, tiled=True)
    tokens = batch * tok
    w0 = weights.reshape(ROWS, 2 * wide)

    up1, down1 = sent(w0, Z_UP), sent(w0, Z_DOWN)
    other0 = sent(w0, Y_OTHER)

    up2, down2 = sent(up1, Z_UP), sent(after(down1, other0), Z_DOWN)
    other_down1 = sent(down1, Y_OTHER)

    up3, down3 = sent(up2, Z_UP), sent(after(down2, other_down1), Z_DOWN)
    other_up1 = sent(up1, Y_OTHER)
    first = stacked(w0, up1, down1, up2, down2)
    first_o = sent(first, CORE_OTHER)

    up4 = sent(up3, Z_UP)
    p_down2 = sent(after(other_down1, down3, other_up1), Z_DOWN)
    other3 = sent(up3, Y_OTHER)
    second = stacked(up3, down3, other0, other_down1, other_up1)
    second_o = sent(second, CORE_OTHER)

    p_up2 = sent(after(other_up1, up4), Z_UP)
    p_down3 = sent(after(p_down2, other3), Z_DOWN)
    other4 = sent(up4, Y_OTHER)
    third = stacked(up4, p_down2, other3)
    third_o = sent(third, CORE_OTHER)

    normed = (norm(place, gains, x.reshape(tokens, 4 * wide)),)
    last = stacked(after(p_up2, *normed), p_down3, other4)
    last_o = sent(last, CORE_OTHER)
    bundles = (last, last_o, first, first_o, second, second_o, third, third_o)
    pieces = [(i * tok, (i + 1) * tok, 0, wide) for i in range(batch - 1)]
    pieces += [(tokens - tok, tokens, 0, wide // 2), (tokens - tok, tokens, wide // 2, wide)]
    front = matmul(normed, 4096, 0, bundles, None, jnp.bfloat16, wide, 0, 256, pieces, 20)
    queries = [sent(piece, TO_ENC) for piece in front]
    back = matmul(normed, 4096, 0, bundles, None, jnp.bfloat16, wide, wide, 256, pieces, 20, 0)

    limit = lengths.reshape(batch)
    shape = (1, batch, tok, 2, wide)
    out, context = None, None
    for (low, _, column, _), query, f, b in zip(pieces, queries, front, back):
        if context is not None:
            query = after(query, context)
        context = attend(low // tok, limit, query, f, b)
        out = finish(low // tok, column, shape, decoder, f, b, sent(context, TO_DEC), out)
    return out


def solution(mesh):
    in_specs = (
        P("section", None, "fsdp", "seq"),
        P("section", None),
        P("section", "fsdp", None, "seq"),
        P(None, "fsdp"),
    )
    out_specs = P("section", None, "fsdp", None, "seq")
    return jax.shard_map(
        per_device, mesh=mesh, in_specs=in_specs, out_specs=out_specs, check_vma=False
    )
```

```python
import functools

import jax
import jax.numpy as jnp
import numpy as np
from jax import lax
from jax.experimental import pallas as pl
from jax.experimental.pallas import tpu as pltpu
from jax.sharding import PartitionSpec as P

HD = 64
AXES = ("section", "fsdp", "seq")
ROWS = 128
MIB = 1024 * 1024


def pairs_of(rule):
    pairs = []
    for s in range(2):
        for z in range(8):
            for y in range(2):
                for c in range(2):
                    for x in range(4):
                        to = rule(s, z, y, c, x)
                        if to is not None:
                            number = lambda s, z, y, c, x: s * 128 + z % 8 * 16 + y * 8 + c * 4 + x % 4
                            pairs.append((number(s, z, y, c, x), number(*to)))
    return pairs


Z_UP = pairs_of(lambda s, z, y, c, x: (s, z + 1, y, c, x))
Z_DOWN = pairs_of(lambda s, z, y, c, x: (s, z - 1, y, c, x))
Y_OTHER = pairs_of(lambda s, z, y, c, x: (s, z, 1 - y, c, x))
CORE_OTHER = pairs_of(lambda s, z, y, c, x: (s, z, y, 1 - c, x))
X_RING = pairs_of(lambda s, z, y, c, x: (s, z, y, c, x + 1 - 2 * c))
TO_ENC = pairs_of(lambda s, z, y, c, x: (0, z, y, c, x) if s == 1 else None)
TO_DEC = pairs_of(lambda s, z, y, c, x: (1, z, y, c, x) if s == 0 else None)


def sent(x, pairs):
    return lax.ppermute(x, AXES, pairs)


def after(x, *others):
    return lax.optimization_barrier((x, *others))[0]


def stack_kernel(*refs):
    parts, out, done = refs[:-2], refs[-2], refs[-1]
    copies, at = [], 0
    for k, part in enumerate(parts):
        copies.append(pltpu.make_async_copy(part, out.at[pl.ds(at, part.shape[0])], done.at[k]))
        at += part.shape[0]
    for copy in copies:
        copy.start()
    for copy in copies:
        copy.wait()


def stacked(*parts):
    return pl.pallas_call(
        stack_kernel,
        in_specs=[pl.BlockSpec(memory_space=pl.ANY)] * len(parts),
        out_specs=pl.BlockSpec(memory_space=pl.ANY),
        out_shape=jax.ShapeDtypeStruct((sum(p.shape[0] for p in parts), parts[0].shape[1]), parts[0].dtype),
        scratch_shapes=[pltpu.SemaphoreType.DMA((len(parts),))],
        compiler_params=pltpu.CompilerParams(vmem_limit_bytes=MIB),
        cost_estimate=pl.CostEstimate(flops=0, bytes_accessed=1024, transcendentals=0),
    )(*parts)


LAST = [(0, 6), (0, 3), (0, 4)]
FIRST = [(1, 0), (1, 7), (1, 1), (1, 6), (1, 2)]
SECOND = [(1, 5), (1, 3), (0, 0), (0, 1), (0, 7)]
THIRD = [(1, 4), (0, 2), (0, 5)]
PLACE = np.zeros((2, 2, 8), np.int32)
_at = 0
for _bundle in (LAST, FIRST, SECOND, THIRD):
    for _own in (1, 0):
        for _same, _far in _bundle:
            PLACE[_same, _own, _far] = _at
            _at += 1


def norm_kernel(group, place_ref, gain_ref, x_ref, out_ref):
    places = [pl.multiple_of(place_ref[k] * ROWS, ROWS) for k in range(32)]

    @pl.loop(0, x_ref.shape[0] // group, unroll=True)
    def _(g):
        at = pl.ds(g * group, group)
        values = [x_ref[at, i * 1024:(i + 1) * 1024].astype(jnp.float32) for i in range(4)]
        squares = (values[0] * values[0] + values[1] * values[1]) + (values[2] * values[2] + values[3] * values[3])
        scale = lax.rsqrt(jnp.sum(squares, axis=-1, keepdims=True) / 4096 + 1e-06)
        for i in range(4):
            normed = (values[i] * scale * gain_ref[:, i * 1024:(i + 1) * 1024]).astype(jnp.bfloat16)
            for b in range(8):
                out_ref[at, pl.ds(places[i * 8 + b], ROWS)] = normed[:, b * ROWS:(b + 1) * ROWS]


def norm(place, gains, x):
    tokens, width = x.shape
    step = 64
    return pl.pallas_call(
        functools.partial(norm_kernel, 32),
        grid_spec=pltpu.PrefetchScalarGridSpec(
            num_scalar_prefetch=1,
            grid=(tokens // step,),
            in_specs=[
                pl.BlockSpec((1, width), lambda i, *_: (0, 0)),
                pl.BlockSpec((step, width), lambda i, *_: (i, 0)),
            ],
            out_specs=pl.BlockSpec((step, width), lambda i, *_: (i, 0)),
        ),
        out_shape=jax.ShapeDtypeStruct((tokens, width), jnp.bfloat16),
        compiler_params=pltpu.CompilerParams(vmem_limit_bytes=6 * MIB),
        cost_estimate=pl.CostEstimate(
            flops=tokens * width * 6, bytes_accessed=tokens * width * 4, transcendentals=tokens
        ),
    )(place, gains, x)


def matmul_kernel(start, n_x, n_parts, has_base, tile, pieces, *refs):
    xs, parts = refs[:n_x], refs[n_x:n_x + n_parts]
    outs, held = refs[n_x + n_parts + has_base:-1], refs[-1]
    j = pl.program_id(0)
    depth = 0
    for part in parts:
        held[depth:depth + part.shape[0], :] = part[...]
        depth += part.shape[0]
    row = 0
    for x in xs:
        count = x.shape[0]
        total = jnp.dot(x[:, start:start + depth], held[...], preferred_element_type=jnp.float32)
        if has_base:
            total = total + refs[n_x + n_parts][row:row + count, :]
        for (low, high, left, right), out in zip(pieces, outs):
            begin, end = max(low, row), min(high, row + count)
            if begin < end:

                @pl.when((j >= left // tile) & (j < right // tile))
                def _():
                    out[begin - low:end - low, :] = total[begin - row:end - row].astype(out.dtype)
        row += count


def matmul(xs, x_block, start, parts, base, dtype, width, column, tile, pieces, mib, weight=1, part=(0, 1)):
    chosen, count = part
    tokens = sum(x.shape[0] for x in xs) // count
    depths = [p.shape[0] for p in parts]
    first = column // tile
    in_specs = [
        pl.BlockSpec((x.shape[0] // count, x_block), lambda j: (chosen, 0), pipeline_mode=pl.Buffered(1)) for x in xs
    ]
    in_specs += [pl.BlockSpec((d, tile), lambda j: (0, first + j)) for d in depths]
    args = [*xs, *parts]
    if base is not None:
        in_specs.append(pl.BlockSpec((tokens, tile), lambda j: (0, first + j)))
        args.append(base)

    def placed(left, right):
        return lambda j: (0, jnp.clip(j - left // tile, 0, (right - left) // tile - 1))

    return pl.pallas_call(
        functools.partial(matmul_kernel, start, len(xs), len(parts), base is not None, tile, pieces),
        grid=(width // tile,),
        in_specs=in_specs,
        out_specs=[pl.BlockSpec((high - low, tile), placed(left, right)) for low, high, left, right in pieces],
        out_shape=[jax.ShapeDtypeStruct((high - low, right - left), dtype) for low, high, left, right in pieces],
        scratch_shapes=[pltpu.VMEM((sum(depths), tile), jnp.bfloat16)],
        compiler_params=pltpu.CompilerParams(vmem_limit_bytes=mib * MIB),
        cost_estimate=pl.CostEstimate(
            flops=weight * 2 * tokens * sum(depths) * width,
            bytes_accessed=weight * (2 * (tokens + width) * sum(depths) + 6 * tokens * width),
            transcendentals=0,
        ),
    )(*args)


def attend_kernel(index, limit_ref, q_ref, k_ref, v_ref, out_ref):
    tok, width = q_ref.shape
    valid = lax.broadcasted_iota(jnp.int32, (tok, tok), 1) < limit_ref[index]
    low = lax.broadcasted_iota(jnp.int32, (tok, 2 * HD), 1) < HD
    for pair in range(width // (2 * HD)):
        cols = slice(pair * 2 * HD, (pair + 1) * 2 * HD)
        q, k, v = q_ref[:, cols], k_ref[:, cols], v_ref[:, cols]
        halves = []
        for mine in (low, ~low):
            scores = lax.dot_general(
                jnp.where(mine, q, jnp.zeros_like(q)), k, (((1,), (1,)), ((), ())), preferred_element_type=jnp.float32
            ) * 0.125
            scores = jnp.where(valid, scores, jnp.float32(-1e30))
            top = jnp.max(scores, axis=-1, keepdims=True)
            e = jnp.exp(scores - top)
            probs = (e * (1.0 / jnp.sum(e, axis=-1, keepdims=True))).astype(jnp.bfloat16)
            halves.append(jnp.dot(probs, v, preferred_element_type=jnp.float32))
        out_ref[:, cols] = jnp.where(low, halves[0], halves[1]).astype(out_ref.dtype)


def attend(index, limit, q, k, v):
    tok, width = q.shape
    whole = pl.BlockSpec((tok, width), lambda i, *_: (0, 0))
    return pl.pallas_call(
        functools.partial(attend_kernel, index),
        grid_spec=pltpu.PrefetchScalarGridSpec(
            num_scalar_prefetch=1, grid=(1,), in_specs=[whole, whole, whole], out_specs=whole
        ),
        out_shape=jax.ShapeDtypeStruct((tok, width), jnp.bfloat16),
        compiler_params=pltpu.CompilerParams(vmem_limit_bytes=8 * MIB),
        cost_estimate=pl.CostEstimate(
            flops=4 * tok * tok * width * 2, bytes_accessed=8 * tok * width, transcendentals=tok * tok * width // HD
        ),
    )(limit, q, k, v)


def finish_kernel(decoder_ref, front_ref, back_ref, context_ref, *refs):
    out_ref = refs[-1]

    @pl.when(decoder_ref[0] == 1)
    def _():
        gate = jax.nn.sigmoid(back_ref[...].astype(jnp.float32))
        out_ref[0, 0, :, 0, :] = (gate * context_ref[...].astype(jnp.float32)).astype(out_ref.dtype)

    @pl.when(decoder_ref[0] != 1)
    def _():
        out_ref[0, 0, :, 0, :] = front_ref[...]

    out_ref[0, 0, :, 1, :] = back_ref[...]


def finish(index, column, shape, decoder, front, back, context, begun):
    tok, width = front.shape
    step = tok // 2
    part = pl.BlockSpec((step, width), lambda i, *_: (i, 0))
    args, in_specs, aliases = [front, back, context], [part, part, part], {}
    if begun is not None:
        args.append(begun)
        in_specs.append(pl.BlockSpec(memory_space=pl.ANY))
        aliases = {4: 0}
    return pl.pallas_call(
        finish_kernel,
        grid_spec=pltpu.PrefetchScalarGridSpec(
            num_scalar_prefetch=1,
            grid=(2,),
            in_specs=in_specs,
            out_specs=pl.BlockSpec((1, 1, step, 2, width), lambda i, *_: (0, index, i, 0, column // width)),
        ),
        out_shape=jax.ShapeDtypeStruct(shape, jnp.bfloat16),
        input_output_aliases=aliases,
        compiler_params=pltpu.CompilerParams(vmem_limit_bytes=6 * MIB),
        cost_estimate=pl.CostEstimate(flops=6 * tok * width, bytes_accessed=10 * tok * width, transcendentals=tok * width),
    )(decoder, *args)


def per_device(inputs, gains, weights, lengths):
    _, batch, tok, wide = inputs.shape
    fsdp, seq = lax.axis_index("fsdp"), lax.axis_index("seq")
    z, y, core = fsdp // 4, fsdp // 2 % 2, fsdp % 2
    decoder = lax.axis_index("section").astype(jnp.int32).reshape(1)

    block = np.arange(32, dtype=np.int32)
    same = (block // 2 % 2 == y).astype(jnp.int32)
    own = (block % 2 == core).astype(jnp.int32)
    place = jnp.asarray(PLACE).reshape(32)[(same * 2 + own) * 8 + (block // 4 - z) % 8]

    x = lax.all_gather(inputs, "seq", axis=3, tiled=True)
    tokens = batch * tok
    w0 = weights.reshape(ROWS, 2 * wide)

    up1, down1 = sent(w0, Z_UP), sent(w0, Z_DOWN)
    other0 = sent(w0, Y_OTHER)

    up2, down2 = sent(up1, Z_UP), sent(after(down1, other0), Z_DOWN)
    other_down1 = sent(down1, Y_OTHER)

    up3, down3 = sent(up2, Z_UP), sent(after(down2, other_down1), Z_DOWN)
    other_up1 = sent(up1, Y_OTHER)
    first = stacked(w0, up1, down1, up2, down2)
    first_o = sent(first, CORE_OTHER)

    up4 = sent(up3, Z_UP)
    p_down2 = sent(after(other_down1, down3, other_up1), Z_DOWN)
    other3 = sent(up3, Y_OTHER)
    second = stacked(up3, down3, other0, other_down1, other_up1)
    second_o = sent(second, CORE_OTHER)

    p_up2 = sent(after(other_up1, up4), Z_UP)
    p_down3 = sent(after(p_down2, other3), Z_DOWN)
    other4 = sent(up4, Y_OTHER)
    third = stacked(up4, p_down2, other3)
    third_o = sent(third, CORE_OTHER)

    normed = (norm(place, gains, x.reshape(tokens, 4 * wide)),)
    last = stacked(after(p_up2, *normed), p_down3, other4)
    last_o = sent(last, CORE_OTHER)
    bundles = (last, last_o, first, first_o, second, second_o, third, third_o)
    pieces = [(i * tok, (i + 1) * tok, 0, wide) for i in range(batch - 1)]
    pieces += [(tokens - tok, tokens, 0, wide // 2), (tokens - tok, tokens, wide // 2, wide)]
    front = matmul(normed, 4096, 0, bundles, None, jnp.bfloat16, wide, 0, 256, pieces, 20)
    queries = [sent(piece, TO_ENC) for piece in front]
    def back_of(x, part, pieces):
        return matmul((x,), 4096, 0, bundles, None, jnp.bfloat16, wide, wide, 256, pieces, 20, 0, (part, 2))

    front, half = list(front), tokens // 2
    back = back_of(normed[0], 0, [p for p in pieces if p[1] <= half])

    limit = lengths.reshape(batch)
    shape = (1, batch, tok, 2, wide)
    out, context = None, None
    for k, (low, _, column, _) in enumerate(pieces):
        query = queries[k]
        if context is not None:
            query = after(query, context)
        if k == 1:
            rest = [(p[0] - half, p[1] - half, *p[2:]) for p in pieces if p[0] >= half]
            back = [*back, *back_of(after(normed[0], context), 1, rest)]
            front[1] = after(front[1], *back)
        context = attend(low // tok, limit, query, front[k], back[k])
        out = finish(low // tok, column, shape, decoder, front[k], back[k], sent(context, TO_DEC), out)
    return out


def solution(mesh):
    in_specs = (
        P("section", None, "fsdp", "seq"),
        P("section", None),
        P("section", "fsdp", None, "seq"),
        P(None, "fsdp"),
    )
    out_specs = P("section", None, "fsdp", None, "seq")
    return jax.shard_map(
        per_device, mesh=mesh, in_specs=in_specs, out_specs=out_specs, check_vma=False
    )
```
